32 devices in a mesh: gx: 2 (over x), gy: 8 (over z, core), gz: 2 (over y).
Axes of the slice: x: 2, y: 2, z: 4, core: 2. Of those that a mesh axis runs over, the one named last changes fastest.
Arguments:
- velocity: float32 [3, 16, 256, 256], P(None, 'gx', 'gy', 'gz'), may hold values from -6 to 6
- fibre_vel: float32 [3, 1048576], P(None, ('gx', 'gy', 'gz')), may hold values from -6 to 6
- fluid_vel: float32 [3, 1048576], P(None, ('gx', 'gy', 'gz')), may hold values from -6 to 6
- fibre_props: float32 [2, 1048576], P(None, ('gx', 'gy', 'gz')), may hold values from 0.2 to 2
- fibre_row: int32 [1048576], P(('gx', 'gy', 'gz')), may hold values from 0 to 255
- fibre_height: int32 [1048576], P(('gx', 'gy', 'gz')), may hold values from 0 to 127
- migrant_list: int32 [4, 32768], P(None, ('gx', 'gy', 'gz')), may hold values from 0 to 32767, as said below
- migrant_slot: int32 [4, 32768], P(None, ('gx', 'gy', 'gz')), may hold values from 0 to 15
- side_rows: int32 [4, 512], P(None, ('gx', 'gy', 'gz')), may hold values from 0 to 255, as said below
Outputs:
- new_velocity: float32 [3, 16, 256, 256], P(None, 'gx', 'gy', 'gz')
- kept_fibres: float32 [3, 1048576], P(None, ('gx', 'gy', 'gz'))
- arrivals: float32 [4, 3, 32768], P(None, None, ('gx', 'gy', 'gz'))
The draws below stay inside these ranges and needn't reach their ends.
Inputs may be any that keep to these rules, and one draw needn't show every extreme that they name: `migrant_list`: the 4096 entries that one brick holds are distinct numbers of fibres of that brick. `side_rows`: row numbers x * 32 + y of the neighbour brick in the list's direction; distinct within one list of one brick. `fibre_row`: A row of the fibre's own brick; not used for a fibre that moves. `migrant_slot`: A slot of the row list of the same direction and brick.
All inputs are finite; a program needn't handle non-finite values.
Results may differ from the reference program's by a relative error of at most 0.00002.
Values sent between devices are 32-bit elements; how exact they have to be, the bound alone decides.
A program may use at most 256 MiB of HBM per device.

```python
import math
import jax
import jax.numpy as jnp
from jax import lax

CX = 8
CY = 32
CZ = 128
FIB_DEV = 32768
MIG = 1024
CAP = 16
SWEEPS = 3
NX = 16
NY = 256
NZ = 256
FIBRES = 1048576
MIGS = 32768
SLOTS = 512
N_GX = 2
N_GY = 8
N_GZ = 2


def pick_distinct(key, groups, pool, count):
    keys = jax.random.split(key, groups)
    picked = jax.vmap(lambda one_key: jax.random.permutation(one_key, pool)[:count])(keys)
    return picked.astype(jnp.int32)


def draw_migrant_list(key, part):
    device_total = MIGS // MIG
    picked = pick_distinct(jax.random.fold_in(key, 11), device_total, FIB_DEV, 4 * MIG)
    return picked.reshape(device_total, 4, MIG).transpose(1, 0, 2).reshape(4, MIGS)


def draw_side_rows(key, part):
    device_total = SLOTS // CAP
    picked = pick_distinct(jax.random.fold_in(key, 23), device_total * 4, CX * CY, CAP)
    return picked.reshape(device_total, 4, CAP).transpose(1, 0, 2).reshape(4, SLOTS)


def set_ends(values, rng, smallest, top_value):
    index_at = [jax.random.randint(jax.random.fold_in(rng, axis), (), 0, length) for axis, length in enumerate(values.shape)]
    widest = values.shape.index(max(values.shape))
    beside = index_at[:widest] + [(index_at[widest] + 1) % values.shape[widest]] + index_at[widest + 1:]
    return values.at[tuple(index_at)].set(smallest).at[tuple(beside)].set(top_value)


def levels(rng, extent, pieces, least, top_value):
    def one(dim, parts):
        draws = jax.random.uniform(jax.random.fold_in(jax.random.fold_in(rng, 6), dim), (parts,), jnp.float32, least / len(pieces), top_value / len(pieces))
        return jnp.repeat(jnp.exp(draws), extent[dim] // parts).reshape((-1,) + (1,) * (len(extent) - dim - 1))

    loudness = one(*pieces[0])
    for cut in pieces[1:]:
        loudness = loudness * one(*cut)
    return loudness


def normal_values(key, extent, width, most, pieces=(), kind=jnp.bfloat16):
    gain = levels(key, extent, pieces, -0.22, 0.18) if pieces else 1.0
    entries = jax.random.normal(key, extent, jnp.float32) * width * gain
    return jnp.minimum(jnp.maximum(entries, -most), most).astype(kind)


def setup_inputs(seed: int = 0) -> dict:
    key_list = jax.random.split(jax.random.key(seed), 10)
    velocity = normal_values(key_list[0], (3, NX, NY, NZ), 1.0, 6.0, ((1, 2), (2, 8), (3, 2)), jnp.float32)
    fibre_vel = normal_values(key_list[1], (3, FIBRES), 1.0, 6.0, ((1, 32),), jnp.float32)
    fluid_vel = normal_values(key_list[2], (3, FIBRES), 1.0, 6.0, ((1, 32),), jnp.float32)
    fibre_props = jnp.clip(jnp.exp(math.log(2.0) - 2.3025851 * jax.random.uniform(key_list[3], (2, FIBRES), jnp.float32) ** levels(key_list[3], (2, FIBRES), ((1, 32),), -0.2, 0.2)), 0.2, 2.0)
    fibre_row = set_ends(jax.random.randint(key_list[4], (FIBRES,), 0, CX * CY), jax.random.fold_in(key_list[4], 1), 0, (CX * CY) - 1).astype(jnp.int32)
    fibre_height = set_ends(jax.random.randint(key_list[5], (FIBRES,), 0, CZ), jax.random.fold_in(key_list[5], 1), 0, CZ - 1).astype(jnp.int32)
    migrant_list = draw_migrant_list(jax.random.fold_in(key_list[9], 71), 0)
    migrant_slot = set_ends(jax.random.randint(key_list[7], (4, MIGS), 0, CAP), jax.random.fold_in(key_list[7], 1), 0, CAP - 1).astype(jnp.int32)
    side_rows = draw_side_rows(jax.random.fold_in(key_list[9], 71), 0)
    return dict(velocity=velocity, fibre_vel=fibre_vel, fluid_vel=fluid_vel, fibre_props=fibre_props, fibre_row=fibre_row, fibre_height=fibre_height, migrant_list=migrant_list, migrant_slot=migrant_slot, side_rows=side_rows)


drag_step = 0.25
source_step = 1.0
coupling = 1.0


def fibre_terms(fibre_vel, fluid_vel, fibre_props):
    volume = fibre_props[0][None, :]
    drag_force = fibre_props[1][None, :] * (fluid_vel - fibre_vel)
    moved_vel = fibre_vel + drag_step * drag_force / volume
    partials = jnp.concatenate([drag_force, volume], axis=0)
    return partials, moved_vel


def adjacent_value(grid_field, axis_location, upper_value):
    leading = grid_field.ndim - 3
    result = grid_field
    for position in range(3):
        length = grid_field.shape[leading + position]
        start = 1
        if position == axis_location:
            start = 2 if upper_value else 0
        result = lax.slice_in_dim(result, start, start + length - 2, axis=leading + position)
    return result


def relaxation_pass(bordered_velocity, bordered_porosity, momentum_source):
    central_value = bordered_porosity[1:-1, 1:-1, 1:-1]
    weight_sum = jnp.zeros_like(central_value)
    flux_sum = jnp.zeros_like(momentum_source)
    for axis_location in range(3):
        for upper_value in (False, True):
            blend_weight = 0.5 * (central_value + adjacent_value(bordered_porosity, axis_location, upper_value))
            weight_sum = weight_sum + blend_weight
            flux_sum = flux_sum + blend_weight[None] * adjacent_value(bordered_velocity, axis_location, upper_value)
    return (momentum_source + coupling * flux_sum) / (central_value + coupling * weight_sum)[None]


def by_device(values, dev_total):
    leading = values.shape[0]
    return values.reshape(leading, dev_total, -1).transpose(1, 0, 2)


def reference(velocity, fibre_vel, fluid_vel, fibre_props, fibre_row, fibre_height, migrant_list, migrant_slot, side_rows):
    grid_shape = (N_GX, N_GY, N_GZ)
    dev_total = N_GX * N_GY * N_GZ
    row_count = CX * CY
    cell_count = row_count * CZ
    vel_dev = by_device(fibre_vel, dev_total)
    fluid_dev = by_device(fluid_vel, dev_total)
    props_dev = by_device(fibre_props, dev_total)
    cell_dev = (fibre_row * CZ + fibre_height).astype(jnp.int32).reshape(dev_total, FIB_DEV)
    height_dev = fibre_height.reshape(dev_total, FIB_DEV)
    list_dev = by_device(migrant_list, dev_total)
    slot_dev = by_device(migrant_slot, dev_total)
    rows_dev = by_device(side_rows, dev_total)

    def local_part(vel_one, fluid_one, props_one, cell_one, height_one, list_one, slot_one):
        partials, moved_vel = fibre_terms(vel_one, fluid_one, props_one)
        staying = jnp.ones((FIB_DEV,), jnp.float32).at[list_one.reshape(-1)].set(0.0)
        kept_vel = moved_vel * staying[None, :]
        deposit = jnp.zeros((4, cell_count), jnp.float32).at[:, cell_one].add(partials * staying[None, :])
        slot_cells = slot_one * CZ + height_one[list_one]
        moving = partials[:, list_one].transpose(1, 0, 2)

        def one_block(cell_ids, part_terms):
            return jnp.zeros((4, CAP * CZ), jnp.float32).at[:, cell_ids].add(part_terms).reshape(4, CAP, CZ)

        blocks = jax.vmap(one_block)(slot_cells, moving)
        movers = moved_vel[:, list_one].transpose(1, 0, 2)
        return kept_vel, deposit, blocks, movers

    kept_vel, deposit, blocks, movers = jax.vmap(local_part)(vel_dev, fluid_dev, props_dev, cell_dev, height_dev, list_dev, slot_dev)

    def add_rows(total_one, rows_one, ids_one):
        return total_one.reshape(4, row_count, CZ).at[:, ids_one].add(rows_one).reshape(4, cell_count)

    arrived = []
    for direction in range(4):
        grid_axis = direction // 2
        step_by = 1 if direction % 2 == 1 else -1

        def neighbour(values):
            spread = values.reshape(grid_shape + values.shape[1:])
            return jnp.roll(spread, step_by, axis=grid_axis).reshape(values.shape)

        got_rows = neighbour(blocks[:, direction])
        got_ids = neighbour(rows_dev[:, direction])
        arrived.append(neighbour(movers[:, direction]))
        deposit = jax.vmap(add_rows)(deposit, got_rows, got_ids)

    field = deposit.reshape(grid_shape + (4, CX, CY, CZ)).transpose(3, 0, 4, 1, 5, 2, 6).reshape(4, NX, NY, NZ)
    void_fraction = 1.0 / (1.0 + field[3])
    momentum_source = void_fraction[None] * velocity - source_step * field[0:3]
    bordered_porosity = jnp.pad(jnp.pad(void_fraction, ((1, 1), (1, 1), (0, 0)), mode="wrap"), ((0, 0), (0, 0), (1, 1)), constant_values=1.0)
    present_velocity = velocity
    for sweep_index in range(SWEEPS):
        bordered_velocity = jnp.pad(jnp.pad(present_velocity, ((0, 0), (1, 1), (1, 1), (0, 0)), mode="wrap"), ((0, 0), (0, 0), (0, 0), (1, 1)))
        present_velocity = relaxation_pass(bordered_velocity, bordered_porosity, momentum_source)
    kept_fibres = kept_vel.transpose(1, 0, 2).reshape(3, FIBRES)
    arrivals = jnp.stack(arrived, axis=0).transpose(0, 2, 1, 3).reshape(4, 3, MIGS)
    return present_velocity, kept_fibres, arrivals
```

```python
import jax
import jax.numpy as jnp
from jax import lax
from jax.experimental import pallas as pl
from jax.experimental.pallas import tpu as pltpu
from jax.sharding import PartitionSpec as P

SWEEPS = 3
drag_step = 0.25
source_step = 1.0
coupling = 1.0
F32, BF16 = jnp.float32, jnp.bfloat16
LANES = 128
GROUP = 16
NT = (((1,), (1,)), ((), ()))


def parts_of(value):
    high = value.astype(BF16)
    low = (value - high.astype(F32)).astype(BF16)
    return high, low


def spread16(row):
    return jnp.broadcast_to(row, (16, row.shape[1])).astype(BF16)


def one_hot(row16, count, iota16):
    blocks = count // 16
    n = row16.shape[1]
    out = []
    for block in range(blocks):
        hit = iota16 == row16 - float(block * 16)
        out.append(jnp.where(hit, jnp.ones((), BF16), jnp.zeros((), BF16)))
    return jnp.concatenate(out, axis=0)


def local_kernel(
    vel, flu, prop, row, height, mlist, mslot, side,
    kept, dep, rows, mov,
    st_vel, st_flu, st_prop, tabs, moved_t, gt_hi, gt_lo, gath, b0, a0, b1, a1, acc,
):
    groups = row.shape[0]
    row_count = dep.shape[1]
    migs = mlist.shape[1]
    slots = side.shape[1]

    def stage(step, carry):
        for k in range(8):
            g = step * 8 + k
            at = pl.multiple_of(g * LANES, LANES)
            to = pl.multiple_of(g * 8, 8)
            st_vel[pl.ds(to, 3), :] = vel[:, pl.ds(at, LANES)]
            st_flu[pl.ds(to, 3), :] = flu[:, pl.ds(at, LANES)]
            st_prop[pl.ds(to, 2), :] = prop[:, pl.ds(at, LANES)]
        return carry

    lax.fori_loop(0, groups // 8, stage, 0)

    lists = mlist[...]
    list_hi = (lists // LANES).astype(F32)
    list_lo = (lists % LANES).astype(F32)
    iota16 = lax.broadcasted_iota(jnp.int32, (16, migs), 0).astype(F32).astype(BF16)
    named = jnp.zeros((groups, LANES), F32)
    for d in range(4):
        named = named + lax.dot_general(
            one_hot(spread16(list_hi[d:d + 1]), groups, iota16),
            one_hot(spread16(list_lo[d:d + 1]), LANES, iota16),
            NT, preferred_element_type=F32,
        )
    leaves = named > 0.5

    volume = st_prop[pl.ds(0, groups, stride=8), :]
    beta = st_prop[pl.ds(1, groups, stride=8), :]
    for c in range(3):
        v = st_vel[pl.ds(c, groups, stride=8), :]
        f = st_flu[pl.ds(c, groups, stride=8), :]
        force = beta * (f - v)
        moved = v + drag_step * force / volume
        st_vel[pl.ds(c, groups, stride=8), :] = jnp.where(leaves, 0.0, moved)
        hi, lo = parts_of(force)
        tabs[c] = hi.astype(F32)
        tabs[4 + c] = lo.astype(F32)
        moved_t[c] = moved
        hi, lo = parts_of(force.T)
        gt_hi[c * LANES:(c + 1) * LANES, :] = hi
        gt_lo[c * LANES:(c + 1) * LANES, :] = lo
        hi, lo = parts_of(moved.T)
        gt_hi[(4 + c) * LANES:(5 + c) * LANES, :] = hi
        gt_lo[(4 + c) * LANES:(5 + c) * LANES, :] = lo
    hi, lo = parts_of(volume)
    tabs[3] = hi.astype(F32)
    tabs[7] = lo.astype(F32)
    hi, lo = parts_of(volume.T)
    gt_hi[3 * LANES:4 * LANES, :] = hi
    gt_lo[3 * LANES:4 * LANES, :] = lo
    hgt = height[...].astype(F32)
    tabs[8] = hgt
    tabs[9] = jnp.where(leaves, -1.0, row[...].astype(F32))
    gt_hi[7 * LANES:8 * LANES, :] = hgt.T.astype(BF16)

    def unstage(step, carry):
        for k in range(8):
            g = step * 8 + k
            at = pl.multiple_of(g * LANES, LANES)
            to = pl.multiple_of(g * 8, 8)
            kept[:, pl.ds(at, LANES)] = st_vel[pl.ds(to, 3), :]
        return carry

    lax.fori_loop(0, groups // 8, unstage, 0)

    chunk = 256
    lane_no = lax.broadcasted_iota(jnp.int32, (LANES, chunk), 0).astype(F32)
    iota_c = iota16[:, :chunk]
    for d in range(4):
        def pick(step, carry):
            at = pl.multiple_of(step * chunk, chunk)
            ids = mlist[d:d + 1, pl.ds(at, chunk)]
            hot = one_hot(spread16((ids // LANES).astype(F32)), groups, iota_c)
            here = lane_no == (ids % LANES).astype(F32)
            got = []
            for f in range(8):
                part = jnp.dot(gt_hi[f * LANES:(f + 1) * LANES, :], hot, preferred_element_type=F32)
                if f < 7:
                    part = part + jnp.dot(
                        gt_lo[f * LANES:(f + 1) * LANES, :], hot, preferred_element_type=F32
                    )
                got.append(jnp.sum(jnp.where(here, part, 0.0), axis=0, keepdims=True))
            gath[:, pl.ds(at, chunk)] = jnp.concatenate(got, axis=0)
            return carry

        lax.fori_loop(0, migs // chunk, pick, 0)
        g8 = gath[...]
        mov[d] = g8[4:7]
        h16 = spread16(g8[7:8])
        hits = [iota16 == h16 - float(16 * block) for block in range(LANES // 16)]
        pieces = []
        for f in range(4):
            pieces.append(parts_of(g8[f:f + 1]))
        for which in range(2):
            for f in range(4):
                v16 = spread16(pieces[f][which].astype(F32))
                for block in range(LANES // 16):
                    base = (which * 4 + f) * LANES + block * 16
                    b0[base:base + 16, :migs] = jnp.where(hits[block], v16, jnp.zeros((), BF16))
        slot_hot = one_hot(spread16(mslot[d:d + 1, :].astype(F32)), slots, iota16)
        block_rows = lax.dot_general(slot_hot, b0[:, :migs], NT, preferred_element_type=F32)
        rows[d, 0:slots, :] = block_rows[:, :4 * LANES] + block_rows[:, 4 * LANES:]
        rows[d, slots:slots + 1, 0:slots] = side[d:d + 1, :].astype(F32)

    iota_l = iota16[:, :LANES]

    def build(group0, b, a):
        for k in range(GROUP):
            g = group0 + k
            cols = slice(k * LANES, (k + 1) * LANES)
            h16 = spread16(tabs[8, pl.ds(g, 1), :])
            r16 = spread16(tabs[9, pl.ds(g, 1), :])
            hits = [iota_l == h16 - float(16 * block) for block in range(LANES // 16)]
            for p in range(8):
                v16 = spread16(tabs[p, pl.ds(g, 1), :])
                for block in range(LANES // 16):
                    base = p * LANES + block * 16
                    b[base:base + 16, cols] = jnp.where(hits[block], v16, jnp.zeros((), BF16))
            for block in range(row_count // 16):
                a[block * 16:(block + 1) * 16, cols] = jnp.where(
                    iota_l == r16 - float(16 * block), jnp.ones((), BF16), jnp.zeros((), BF16)
                )

    def add(b, a):
        acc[...] += lax.dot_general(b[...], a[...], NT, preferred_element_type=F32)

    acc[...] = jnp.zeros_like(acc)
    build(0, b0, a0)
    pairs = groups // (2 * GROUP)

    def deposit(step, carry):
        build(step * 2 * GROUP + GROUP, b1, a1)
        add(b0, a0)
        build(jnp.minimum(step + 1, pairs - 1) * 2 * GROUP, b0, a0)
        add(b1, a1)
        return carry

    lax.fori_loop(0, pairs, deposit, 0)
    for f in range(4):
        total = acc[f * LANES:(f + 1) * LANES, :] + acc[(4 + f) * LANES:(5 + f) * LANES, :]
        dep[f] = total.T


def local_part(fibre_vel, fluid_vel, fibre_props, fibre_row, fibre_height, migrant_list, migrant_slot, side_rows, row_count):
    fibres = fibre_vel.shape[1]
    groups = fibres // LANES
    migs = migrant_list.shape[1]
    slots = side_rows.shape[1]
    wide = GROUP * LANES
    vm = pl.BlockSpec(memory_space=pltpu.VMEM)
    return pl.pallas_call(
        local_kernel,
        out_shape=(
            jax.ShapeDtypeStruct((3, fibres), F32),
            jax.ShapeDtypeStruct((4, row_count, LANES), F32),
            jax.ShapeDtypeStruct((4, slots + 8, 4 * LANES), F32),
            jax.ShapeDtypeStruct((4, 3, migs), F32),
        ),
        in_specs=[vm] * 8,
        out_specs=(vm,) * 4,
        scratch_shapes=[
            pltpu.VMEM((groups * 8, LANES), F32),
            pltpu.VMEM((groups * 8, LANES), F32),
            pltpu.VMEM((groups * 8, LANES), F32),
            pltpu.VMEM((10, groups, LANES), F32),
            pltpu.VMEM((3, groups, LANES), F32),
            pltpu.VMEM((8 * LANES, groups), BF16),
            pltpu.VMEM((7 * LANES, groups), BF16),
            pltpu.VMEM((8, migs), F32),
            pltpu.VMEM((8 * LANES, wide), BF16),
            pltpu.VMEM((row_count, wide), BF16),
            pltpu.VMEM((8 * LANES, wide), BF16),
            pltpu.VMEM((row_count, wide), BF16),
            pltpu.VMEM((8 * LANES, row_count), F32),
        ],
        compiler_params=pltpu.CompilerParams(vmem_limit_bytes=56 * 1024 * 1024),
        cost_estimate=pl.CostEstimate(flops=17_000_000_000, bytes_accessed=3_000_000, transcendentals=0),
        name="fibres",
    )(
        fibre_vel, fluid_vel, fibre_props,
        fibre_row.reshape(groups, LANES), fibre_height.reshape(groups, LANES),
        migrant_list, migrant_slot, side_rows,
    )


def passed_along(value, axis, steps):
    count = lax.axis_size(axis)
    pairs = [(source, (source + steps) % count) for source in range(count)]
    return lax.ppermute(value, axis, pairs)


def padded(array, sides, width):
    for axis, dim in sides:
        devices, length = (lax.axis_size(axis), array.shape[dim])
        up = [(i, (i + 1) % devices) for i in range(devices)]
        down = [(j, i) for i, j in up]
        last = lax.slice_in_dim(array, length - width, length, axis=dim)
        leading = lax.slice_in_dim(array, 0, width, axis=dim)
        before = lax.ppermute(last, axis, up)
        after = lax.ppermute(leading, axis, down)
        array = jnp.concatenate([before, array, after], axis=dim)
    return array


def fibre_terms(fibre_vel, fluid_vel, fibre_props):
    volume = fibre_props[0][None, :]
    drag_force = fibre_props[1][None, :] * (fluid_vel - fibre_vel)
    moved_vel = fibre_vel + drag_step * drag_force / volume
    partials = jnp.concatenate([drag_force, volume], axis=0)
    return (partials, moved_vel)


def adjacent_value(grid_field, axis_location, upper_value):
    leading = grid_field.ndim - 3
    result = grid_field
    for position in range(3):
        length = grid_field.shape[leading + position]
        start = 1
        if position == axis_location:
            start = 2 if upper_value else 0
        result = lax.slice_in_dim(result, start, start + length - 2, axis=leading + position)
    return result


def relaxation_pass(bordered_velocity, bordered_porosity, momentum_source):
    central_value = bordered_porosity[1:-1, 1:-1, 1:-1]
    weight_sum = jnp.zeros_like(central_value)
    flux_sum = jnp.zeros_like(momentum_source)
    for axis_location in range(3):
        for upper_value in (False, True):
            blend_weight = 0.5 * (
                central_value + adjacent_value(bordered_porosity, axis_location, upper_value)
            )
            weight_sum = weight_sum + blend_weight
            flux_sum = flux_sum + blend_weight[None] * adjacent_value(
                bordered_velocity, axis_location, upper_value
            )
    return (momentum_source + coupling * flux_sum) / (central_value + coupling * weight_sum)[None]


def wall_cells(brick_depth, margin):
    heights = (
        lax.axis_index("gz") * brick_depth
        + jnp.arange(brick_depth + 2 * margin, dtype=jnp.int32)
        - margin
    )
    return (heights < 0) | (heights >= brick_depth * lax.axis_size("gz"))


def body(
    velocity,
    fibre_vel,
    fluid_vel,
    fibre_props,
    fibre_row,
    fibre_height,
    migrant_list,
    migrant_slot,
    side_rows,
):
    width_x, width_y, width_z = (velocity.shape[1], velocity.shape[2], velocity.shape[3])
    row_count = width_x * width_y
    cell_count = row_count * width_z
    slot_count = side_rows.shape[1]
    kept_fibres, deposit, rows, movers = local_part(
        fibre_vel, fluid_vel, fibre_props, fibre_row, fibre_height,
        migrant_list, migrant_slot, side_rows, row_count,
    )
    arrived = []
    for direction in range(4):
        step_by = 1 if direction % 2 == 1 else -1
        got_rows, got_vel = passed_along(
            (rows[direction], movers[direction]), "gx" if direction < 2 else "gy", step_by
        )
        got_ids = got_rows[slot_count, :slot_count].astype(jnp.int32)
        moved_rows = got_rows[:slot_count].reshape(slot_count, 4, width_z).transpose(1, 0, 2)
        deposit = deposit.at[:, got_ids].add(moved_rows)
        arrived.append(got_vel)
    drag_field = deposit[0:3].reshape(3, width_x, width_y, width_z)
    void_fraction = 1.0 / (1.0 + deposit[3].reshape(width_x, width_y, width_z))
    momentum_source = void_fraction[None] * velocity - source_step * drag_field
    boundary_mask = wall_cells(width_z, 1)
    bordered_field = padded(
        jnp.concatenate([velocity, void_fraction[None]], axis=0),
        (("gx", 1), ("gy", 2), ("gz", 3)),
        1,
    )
    bordered_porosity = jnp.where(boundary_mask, 1.0, bordered_field[3])
    present_velocity = relaxation_pass(
        jnp.where(boundary_mask, 0.0, bordered_field[0:3]), bordered_porosity, momentum_source
    )
    for sweep_index in range(SWEEPS - 1):
        bordered_velocity = padded(present_velocity, (("gx", 1), ("gy", 2), ("gz", 3)), 1)
        present_velocity = relaxation_pass(
            jnp.where(boundary_mask, 0.0, bordered_velocity), bordered_porosity, momentum_source
        )
    arrivals = jnp.stack(arrived, axis=0)
    return (present_velocity, kept_fibres, arrivals)


def solution(mesh):
    placed = (
        P(None, "gx", "gy", "gz"),
        P(None, ("gx", "gy", "gz")),
        P(None, ("gx", "gy", "gz")),
        P(None, ("gx", "gy", "gz")),
        P(("gx", "gy", "gz")),
        P(("gx", "gy", "gz")),
        P(None, ("gx", "gy", "gz")),
        P(None, ("gx", "gy", "gz")),
        P(None, ("gx", "gy", "gz")),
    )
    return jax.shard_map(
        body,
        mesh=mesh,
        in_specs=placed,
        out_specs=(
            P(None, "gx", "gy", "gz"),
            P(None, ("gx", "gy", "gz")),
            P(None, None, ("gx", "gy", "gz")),
        ),
        check_vma=False,
    )
```

```python
import jax
import jax.numpy as jnp
from jax import lax
from jax.experimental import pallas as pl
from jax.experimental.pallas import tpu as pltpu
from jax.sharding import PartitionSpec as P

SWEEPS = 3
drag_step = 0.25
source_step = 1.0
coupling = 1.0
F32, BF16 = jnp.float32, jnp.bfloat16
LANES = 128
GROUP = 16
NT = (((1,), (1,)), ((), ()))


def parts_of(value):
    high = value.astype(BF16)
    low = (value - high.astype(F32)).astype(BF16)
    return high, low


def spread16(row):
    return jnp.broadcast_to(row, (16, row.shape[1])).astype(BF16)


def one_hot(row16, count, iota16):
    blocks = count // 16
    n = row16.shape[1]
    out = []
    for block in range(blocks):
        hit = iota16 == row16 - float(block * 16)
        out.append(jnp.where(hit, jnp.ones((), BF16), jnp.zeros((), BF16)))
    return jnp.concatenate(out, axis=0)


def local_kernel(
    vel, flu, prop, row, height, mlist, mslot, side,
    kept, dep, rows, mov,
    st_vel, st_flu, st_prop, tabs, moved_t, gt_hi, gt_lo, gath, b0, a0, b1, a1, acc,
):
    groups = row.shape[0]
    row_count = dep.shape[1]
    migs = mlist.shape[1]
    slots = side.shape[1]

    def stage(step, carry):
        for k in range(8):
            g = step * 8 + k
            at = pl.multiple_of(g * LANES, LANES)
            to = pl.multiple_of(g * 8, 8)
            st_vel[pl.ds(to, 3), :] = vel[:, pl.ds(at, LANES)]
            st_flu[pl.ds(to, 3), :] = flu[:, pl.ds(at, LANES)]
            st_prop[pl.ds(to, 2), :] = prop[:, pl.ds(at, LANES)]
        return carry

    lax.fori_loop(0, groups // 8, stage, 0)

    lists = mlist[...]
    list_hi = (lists // LANES).astype(F32)
    list_lo = (lists % LANES).astype(F32)
    iota16 = lax.broadcasted_iota(jnp.int32, (16, migs), 0).astype(F32).astype(BF16)
    named = jnp.zeros((groups, LANES), F32)
    for d in range(4):
        named = named + lax.dot_general(
            one_hot(spread16(list_hi[d:d + 1]), groups, iota16),
            one_hot(spread16(list_lo[d:d + 1]), LANES, iota16),
            NT, preferred_element_type=F32,
        )
    leaves = named > 0.5

    volume = st_prop[pl.ds(0, groups, stride=8), :]
    beta = st_prop[pl.ds(1, groups, stride=8), :]
    for c in range(3):
        v = st_vel[pl.ds(c, groups, stride=8), :]
        f = st_flu[pl.ds(c, groups, stride=8), :]
        force = beta * (f - v)
        moved = v + drag_step * force / volume
        st_vel[pl.ds(c, groups, stride=8), :] = jnp.where(leaves, 0.0, moved)
        hi, lo = parts_of(force)
        tabs[c] = hi.astype(F32)
        tabs[4 + c] = lo.astype(F32)
        moved_t[c] = moved
        hi, lo = parts_of(force.T)
        gt_hi[c * LANES:(c + 1) * LANES, :] = hi
        gt_lo[c * LANES:(c + 1) * LANES, :] = lo
        hi, lo = parts_of(moved.T)
        gt_hi[(4 + c) * LANES:(5 + c) * LANES, :] = hi
        gt_lo[(4 + c) * LANES:(5 + c) * LANES, :] = lo
    hi, lo = parts_of(volume)
    tabs[3] = hi.astype(F32)
    tabs[7] = lo.astype(F32)
    hi, lo = parts_of(volume.T)
    gt_hi[3 * LANES:4 * LANES, :] = hi
    gt_lo[3 * LANES:4 * LANES, :] = lo
    hgt = height[...].astype(F32)
    tabs[8] = hgt
    tabs[9] = jnp.where(leaves, -1.0, row[...].astype(F32))
    gt_hi[7 * LANES:8 * LANES, :] = hgt.T.astype(BF16)

    def unstage(step, carry):
        for k in range(8):
            g = step * 8 + k
            at = pl.multiple_of(g * LANES, LANES)
            to = pl.multiple_of(g * 8, 8)
            kept[:, pl.ds(at, LANES)] = st_vel[pl.ds(to, 3), :]
        return carry

    lax.fori_loop(0, groups // 8, unstage, 0)

    chunk = 256
    lane_no = lax.broadcasted_iota(jnp.int32, (LANES, chunk), 0).astype(F32)
    iota_c = iota16[:, :chunk]
    for d in range(4):
        def pick(step, carry):
            at = pl.multiple_of(step * chunk, chunk)
            ids = mlist[d:d + 1, pl.ds(at, chunk)]
            hot = one_hot(spread16((ids // LANES).astype(F32)), groups, iota_c)
            here = lane_no == (ids % LANES).astype(F32)
            got = []
            for f in range(8):
                part = jnp.dot(gt_hi[f * LANES:(f + 1) * LANES, :], hot, preferred_element_type=F32)
                if f < 7:
                    part = part + jnp.dot(
                        gt_lo[f * LANES:(f + 1) * LANES, :], hot, preferred_element_type=F32
                    )
                got.append(jnp.sum(jnp.where(here, part, 0.0), axis=0, keepdims=True))
            gath[:, pl.ds(at, chunk)] = jnp.concatenate(got, axis=0)
            return carry

        lax.fori_loop(0, migs // chunk, pick, 0)
        g8 = gath[...]
        mov[d] = g8[4:7]
        h16 = spread16(g8[7:8])
        hits = [iota16 == h16 - float(16 * block) for block in range(LANES // 16)]
        pieces = []
        for f in range(4):
            pieces.append(parts_of(g8[f:f + 1]))
        for which in range(2):
            for f in range(4):
                v16 = spread16(pieces[f][which].astype(F32))
                for block in range(LANES // 16):
                    base = (which * 4 + f) * LANES + block * 16
                    b0[base:base + 16, :migs] = jnp.where(hits[block], v16, jnp.zeros((), BF16))
        slot_hot = one_hot(spread16(mslot[d:d + 1, :].astype(F32)), slots, iota16)
        block_rows = lax.dot_general(slot_hot, b0[:, :migs], NT, preferred_element_type=F32)
        rows[d, 0:slots, :] = block_rows[:, :4 * LANES] + block_rows[:, 4 * LANES:]
        rows[d, slots:slots + 1, 0:slots] = side[d:d + 1, :].astype(F32)

    iota_l = iota16[:, :LANES]

    def build(group0, b, a):
        for k in range(GROUP):
            g = group0 + k
            cols = slice(k * LANES, (k + 1) * LANES)
            h16 = spread16(tabs[8, pl.ds(g, 1), :])
            r16 = spread16(tabs[9, pl.ds(g, 1), :])
            hits = [iota_l == h16 - float(16 * block) for block in range(LANES // 16)]
            for p in range(8):
                v16 = spread16(tabs[p, pl.ds(g, 1), :])
                for block in range(LANES // 16):
                    base = p * LANES + block * 16
                    b[base:base + 16, cols] = jnp.where(hits[block], v16, jnp.zeros((), BF16))
            for block in range(row_count // 16):
                a[block * 16:(block + 1) * 16, cols] = jnp.where(
                    iota_l == r16 - float(16 * block), jnp.ones((), BF16), jnp.zeros((), BF16)
                )

    def add(b, a):
        acc[...] += lax.dot_general(b[...], a[...], NT, preferred_element_type=F32)

    acc[...] = jnp.zeros_like(acc)
    build(0, b0, a0)
    pairs = groups // (2 * GROUP)

    def deposit(step, carry):
        build(step * 2 * GROUP + GROUP, b1, a1)
        add(b0, a0)
        build(jnp.minimum(step + 1, pairs - 1) * 2 * GROUP, b0, a0)
        add(b1, a1)
        return carry

    lax.fori_loop(0, pairs, deposit, 0)
    for f in range(4):
        total = acc[f * LANES:(f + 1) * LANES, :] + acc[(4 + f) * LANES:(5 + f) * LANES, :]
        dep[f] = total.T


def local_part(fibre_vel, fluid_vel, fibre_props, fibre_row, fibre_height, migrant_list, migrant_slot, side_rows, row_count):
    fibres = fibre_vel.shape[1]
    groups = fibres // LANES
    migs = migrant_list.shape[1]
    slots = side_rows.shape[1]
    wide = GROUP * LANES
    vm = pl.BlockSpec(memory_space=pltpu.VMEM)
    return pl.pallas_call(
        local_kernel,
        out_shape=(
            jax.ShapeDtypeStruct((3, fibres), F32),
            jax.ShapeDtypeStruct((4, row_count, LANES), F32),
            jax.ShapeDtypeStruct((4, slots + 8, 4 * LANES), F32),
            jax.ShapeDtypeStruct((4, 3, migs), F32),
        ),
        in_specs=[vm] * 8,
        out_specs=(vm,) * 4,
        scratch_shapes=[
            pltpu.VMEM((groups * 8, LANES), F32),
            pltpu.VMEM((groups * 8, LANES), F32),
            pltpu.VMEM((groups * 8, LANES), F32),
            pltpu.VMEM((10, groups, LANES), F32),
            pltpu.VMEM((3, groups, LANES), F32),
            pltpu.VMEM((8 * LANES, groups), BF16),
            pltpu.VMEM((7 * LANES, groups), BF16),
            pltpu.VMEM((8, migs), F32),
            pltpu.VMEM((8 * LANES, wide), BF16),
            pltpu.VMEM((row_count, wide), BF16),
            pltpu.VMEM((8 * LANES, wide), BF16),
            pltpu.VMEM((row_count, wide), BF16),
            pltpu.VMEM((8 * LANES, row_count), F32),
        ],
        compiler_params=pltpu.CompilerParams(vmem_limit_bytes=56 * 1024 * 1024),
        cost_estimate=pl.CostEstimate(flops=17_000_000_000, bytes_accessed=3_000_000, transcendentals=0),
        name="fibres",
    )(
        fibre_vel, fluid_vel, fibre_props,
        fibre_row.reshape(groups, LANES), fibre_height.reshape(groups, LANES),
        migrant_list, migrant_slot, side_rows,
    )


MESH = pl.DeviceIdType.MESH


def sweep_kernel(
    velocity, dep, rows, mov,
    out, arrivals,
    got_rows, got_mov, u1, u2, phi, src, wts, inv, sy, sz, hx, hy, hz,
    row_send, row_recv, mov_send, mov_recv, face_send, face_recv,
):
    wide_x, wide_y = velocity.shape[1], velocity.shape[2]
    slots = rows.shape[1] - 8
    near = []
    for axis in ("gx", "gy", "gz"):
        n = lax.axis_size(axis)
        me = lax.axis_index(axis)
        near.append({axis: lax.rem(me + n - 1, n)})
        near.append({axis: lax.rem(me + 1, n)})

    barrier = pltpu.get_barrier_semaphore()
    for device in near:
        pl.semaphore_signal(barrier, inc=1, device_id=device, device_id_type=MESH)
    pl.semaphore_wait(barrier, 6)

    copies = []

    def send(source, target, send_sem, recv_sem, device):
        copy = pltpu.make_async_remote_copy(
            src_ref=source, dst_ref=target, send_sem=send_sem, recv_sem=recv_sem,
            device_id=device, device_id_type=MESH,
        )
        copy.start()
        copies.append(copy)
        return copy

    row_copies = [
        send(rows.at[d], got_rows.at[d], row_send.at[d], row_recv.at[d], near[d]) for d in range(4)
    ]

    sub = lax.broadcasted_iota(jnp.int32, (wide_y, LANES), 0)
    lane = lax.broadcasted_iota(jnp.int32, (wide_y, LANES), 1)

    def send_faces(phase, field, count):
        total = count * wide_x
        started = []
        started.append(send(
            field.at[:, 0], hx.at[phase, 1, pl.ds(0, count)],
            face_send.at[phase, 0], face_recv.at[phase, 1], near[0],
        ))
        started.append(send(
            field.at[:, wide_x - 1], hx.at[phase, 0, pl.ds(0, count)],
            face_send.at[phase, 1], face_recv.at[phase, 0], near[1],
        ))
        low = jnp.zeros((wide_y, LANES), F32)
        high = jnp.zeros((wide_y, LANES), F32)
        for j in range(total):
            plane = field[j // wide_x, j % wide_x]
            sy[phase, 0, j:j + 1, :] = plane[0:1, :]
            sy[phase, 1, j:j + 1, :] = plane[wide_y - 1:wide_y, :]
            low = jnp.where(lane == j, pltpu.roll(plane, j, 1) if j else plane, low)
            high = jnp.where(lane == j, pltpu.roll(plane, j + 1, 1), high)
        for side in range(2):
            started.append(send(
                sy.at[phase, side, pl.ds(0, total)], hy.at[phase, 1 - side, pl.ds(0, total)],
                face_send.at[phase, 2 + side], face_recv.at[phase, 3 - side], near[2 + side],
            ))
        sz[phase, 0] = low
        sz[phase, 1] = high
        for side in range(2):
            started.append(send(
                sz.at[phase, side], hz.at[phase, 1 - side],
                face_send.at[phase, 4 + side], face_recv.at[phase, 5 - side], near[4 + side],
            ))
        return started

    def arrive(started):
        for copy in started:
            copy.wait_recv()

    bottom = lax.axis_index("gz") == 0
    top = lax.axis_index("gz") == lax.axis_size("gz") - 1

    def z_halos(phase, wall):
        return (
            jnp.where(bottom, wall, hz[phase, 0]),
            jnp.where(top, wall, hz[phase, 1]),
        )

    def around(phase, field, c, x, z_low, z_high):
        j = c * wide_x + x
        here = field[c, x]
        x_low = field[c, x - 1] if x > 0 else hx[phase, 0, c]
        x_high = field[c, x + 1] if x < wide_x - 1 else hx[phase, 1, c]
        y_low = jnp.where(sub == 0, hy[phase, 0, j:j + 1, :], pltpu.roll(here, 1, 0))
        y_high = jnp.where(
            sub == wide_y - 1, hy[phase, 1, j:j + 1, :], pltpu.roll(here, wide_y - 1, 0)
        )
        edge_low = pltpu.roll(z_low, LANES - j, 1) if j else z_low
        edge_high = pltpu.roll(z_high, LANES - 1 - j, 1)
        below = jnp.where(lane == 0, edge_low, pltpu.roll(here, 1, 1))
        above = jnp.where(lane == LANES - 1, edge_high, pltpu.roll(here, LANES - 1, 1))
        return here, (x_low, x_high, y_low, y_high, below, above)

    first = send_faces(0, velocity, 3)
    mov_copies = [
        send(mov.at[d], got_mov.at[d], mov_send.at[d], mov_recv.at[d], near[d]) for d in range(4)
    ]

    extra = jnp.zeros((wide_x * wide_y, 4 * LANES), F32)
    row_no = lax.broadcasted_iota(jnp.int32, (wide_x * wide_y, slots), 0).astype(F32)
    for d in range(4):
        row_copies[d].wait_recv()
        ids = got_rows[d, slots:slots + 1, 0:slots]
        hot = jnp.where(row_no == ids, 1.0, 0.0).astype(BF16)
        hi, lo = parts_of(got_rows[d, 0:slots, :])
        extra = extra + jnp.dot(hot, hi, preferred_element_type=F32)
        extra = extra + jnp.dot(hot, lo, preferred_element_type=F32)
    fraction = 1.0 / (1.0 + (dep[3] + extra[:, 3 * LANES:]))
    phi[...] = fraction.reshape(1, wide_x, wide_y, LANES)
    second = send_faces(1, phi, 1)
    for c in range(3):
        drag = (dep[c] + extra[:, c * LANES:(c + 1) * LANES]).reshape(wide_x, wide_y, LANES)
        src[c] = phi[0] * velocity[c] - source_step * drag

    arrive(second)
    z_low, z_high = z_halos(1, 1.0)
    for x in range(wide_x):
        here, others = around(1, phi, 0, x, z_low, z_high)
        total = jnp.zeros_like(here)
        for k in range(6):
            weight = 0.5 * (here + others[k])
            wts[k, x] = weight
            total = total + weight
        inv[x] = 1.0 / (here + coupling * total)

    def sweep(phase, field, target):
        z_low, z_high = z_halos(phase, 0.0)
        for x in range(wide_x):
            for c in range(3):
                here, others = around(phase, field, c, x, z_low, z_high)
                flux = wts[0, x] * others[0]
                for k in range(1, 6):
                    flux = flux + wts[k, x] * others[k]
                target[c, x] = (src[c, x] + coupling * flux) * inv[x]

    arrive(first)
    sweep(0, velocity, u1)
    third = send_faces(2, u1, 3)
    for d in range(4):
        mov_copies[d].wait_recv()
        arrivals[d] = got_mov[d]
    arrive(third)
    sweep(2, u1, u2)
    fourth = send_faces(3, u2, 3)
    arrive(fourth)
    sweep(3, u2, out)
    for copy in copies:
        copy.wait_send()


def sweeps(velocity, deposit, rows, movers):
    _, wide_x, wide_y, wide_z = velocity.shape
    vm = pl.BlockSpec(memory_space=pltpu.VMEM)
    sem = pltpu.SemaphoreType.DMA
    field = (3, wide_x, wide_y, wide_z)
    return pl.pallas_call(
        sweep_kernel,
        out_shape=(
            jax.ShapeDtypeStruct(velocity.shape, F32),
            jax.ShapeDtypeStruct(movers.shape, F32),
        ),
        in_specs=[vm] * 4,
        out_specs=(vm,) * 2,
        scratch_shapes=[
            pltpu.VMEM(rows.shape, F32),
            pltpu.VMEM(movers.shape, F32),
            pltpu.VMEM(field, F32),
            pltpu.VMEM(field, F32),
            pltpu.VMEM((1,) + field[1:], F32),
            pltpu.VMEM(field, F32),
            pltpu.VMEM((6,) + field[1:], F32),
            pltpu.VMEM(field[1:], F32),
            pltpu.VMEM((4, 2, 3 * wide_x, wide_z), F32),
            pltpu.VMEM((4, 2, wide_y, wide_z), F32),
            pltpu.VMEM((4, 2, 3, wide_y, wide_z), F32),
            pltpu.VMEM((4, 2, 3 * wide_x, wide_z), F32),
            pltpu.VMEM((4, 2, wide_y, wide_z), F32),
            sem((4,)), sem((4,)), sem((4,)), sem((4,)), sem((4, 6)), sem((4, 6)),
        ],
        compiler_params=pltpu.CompilerParams(
            collective_id=0, has_side_effects=True, vmem_limit_bytes=32 * 1024 * 1024
        ),
        cost_estimate=pl.CostEstimate(flops=20_000_000, bytes_accessed=2_000_000, transcendentals=0),
        name="sweeps",
    )(velocity, deposit, rows, movers)


def body(
    velocity, fibre_vel, fluid_vel, fibre_props, fibre_row, fibre_height,
    migrant_list, migrant_slot, side_rows,
):
    row_count = velocity.shape[1] * velocity.shape[2]
    kept_fibres, deposit, rows, movers = local_part(
        fibre_vel, fluid_vel, fibre_props, fibre_row, fibre_height,
        migrant_list, migrant_slot, side_rows, row_count,
    )
    new_velocity, arrivals = sweeps(velocity, deposit, rows, movers)
    return new_velocity, kept_fibres, arrivals


def solution(mesh):
    placed = (
        P(None, "gx", "gy", "gz"),
        P(None, ("gx", "gy", "gz")),
        P(None, ("gx", "gy", "gz")),
        P(None, ("gx", "gy", "gz")),
        P(("gx", "gy", "gz")),
        P(("gx", "gy", "gz")),
        P(None, ("gx", "gy", "gz")),
        P(None, ("gx", "gy", "gz")),
        P(None, ("gx", "gy", "gz")),
    )
    return jax.shard_map(
        body,
        mesh=mesh,
        in_specs=placed,
        out_specs=(
            P(None, "gx", "gy", "gz"),
            P(None, ("gx", "gy", "gz")),
            P(None, None, ("gx", "gy", "gz")),
        ),
        check_vma=False,
    )
```

```python
import jax
import jax.numpy as jnp
from jax import lax
from jax.experimental import pallas as pl
from jax.experimental.pallas import tpu as pltpu
from jax.sharding import PartitionSpec as P

SWEEPS = 3
drag_step = 0.25
source_step = 1.0
coupling = 1.0
F32, BF16 = jnp.float32, jnp.bfloat16
LANES = 128
GROUP = 16
NT = (((1,), (1,)), ((), ()))


def parts_of(value):
    high = value.astype(BF16)
    low = (value - high.astype(F32)).astype(BF16)
    return high, low


def spread16(row):
    return jnp.broadcast_to(row, (16, row.shape[1])).astype(BF16)


def one_hot(row16, count, iota16):
    blocks = count // 16
    n = row16.shape[1]
    out = []
    for block in range(blocks):
        hit = iota16 == row16 - float(block * 16)
        out.append(jnp.where(hit, jnp.ones((), BF16), jnp.zeros((), BF16)))
    return jnp.concatenate(out, axis=0)


MESH = pl.DeviceIdType.MESH


def step_kernel(
    velocity, vel, flu, prop, row, height, mlist, mslot, side,
    out, kept, arrivals,
    st_vel, st_flu, st_prop, tabs, gt_hi, gt_lo, gath, b0, a0, b1, a1, acc, dep, rows, mov,
    got_rows, got_mov, u1, u2, phi, src, wts, inv, sy, sz, hx, hy, hz,
    row_send, row_recv, mov_send, mov_recv, face_send, face_recv,
):
    wide_x, wide_y = velocity.shape[1], velocity.shape[2]
    near = []
    for axis in ("gx", "gy", "gz"):
        n = lax.axis_size(axis)
        me = lax.axis_index(axis)
        near.append({axis: lax.rem(me + n - 1, n)})
        near.append({axis: lax.rem(me + 1, n)})

    barrier = pltpu.get_barrier_semaphore()
    for device in near:
        pl.semaphore_signal(barrier, inc=1, device_id=device, device_id_type=MESH)

    groups = row.shape[0]
    row_count = wide_x * wide_y
    migs = mlist.shape[1]
    slots = side.shape[1]

    def stage(step, carry):
        for k in range(8):
            g = step * 8 + k
            at = pl.multiple_of(g * LANES, LANES)
            to = pl.multiple_of(g * 8, 8)
            st_vel[pl.ds(to, 3), :] = vel[:, pl.ds(at, LANES)]
            st_flu[pl.ds(to, 3), :] = flu[:, pl.ds(at, LANES)]
            st_prop[pl.ds(to, 2), :] = prop[:, pl.ds(at, LANES)]
        return carry

    lax.fori_loop(0, groups // 8, stage, 0)

    lists = mlist[...]
    list_hi = (lists // LANES).astype(F32)
    list_lo = (lists % LANES).astype(F32)
    iota16 = lax.broadcasted_iota(jnp.int32, (16, migs), 0).astype(F32).astype(BF16)
    named = jnp.zeros((groups, LANES), F32)
    for d in range(4):
        named = named + lax.dot_general(
            one_hot(spread16(list_hi[d:d + 1]), groups, iota16),
            one_hot(spread16(list_lo[d:d + 1]), LANES, iota16),
            NT, preferred_element_type=F32,
        )
    leaves = named > 0.5

    volume = st_prop[pl.ds(0, groups, stride=8), :]
    beta = st_prop[pl.ds(1, groups, stride=8), :]
    for c in range(3):
        v = st_vel[pl.ds(c, groups, stride=8), :]
        f = st_flu[pl.ds(c, groups, stride=8), :]
        force = beta * (f - v)
        moved = v + drag_step * force / volume
        st_vel[pl.ds(c, groups, stride=8), :] = jnp.where(leaves, 0.0, moved)
        hi, lo = parts_of(force)
        tabs[c] = hi.astype(F32)
        tabs[4 + c] = lo.astype(F32)
        hi, lo = parts_of(force.T)
        gt_hi[c * LANES:(c + 1) * LANES, :] = hi
        gt_lo[c * LANES:(c + 1) * LANES, :] = lo
        hi, lo = parts_of(moved.T)
        gt_hi[(4 + c) * LANES:(5 + c) * LANES, :] = hi
        gt_lo[(4 + c) * LANES:(5 + c) * LANES, :] = lo
    hi, lo = parts_of(volume)
    tabs[3] = hi.astype(F32)
    tabs[7] = lo.astype(F32)
    hi, lo = parts_of(volume.T)
    gt_hi[3 * LANES:4 * LANES, :] = hi
    gt_lo[3 * LANES:4 * LANES, :] = lo
    hgt = height[...].astype(F32)
    tabs[8] = hgt
    tabs[9] = jnp.where(leaves, -1.0, row[...].astype(F32))
    gt_hi[7 * LANES:8 * LANES, :] = hgt.T.astype(BF16)

    def unstage(step, carry):
        for k in range(8):
            g = step * 8 + k
            at = pl.multiple_of(g * LANES, LANES)
            to = pl.multiple_of(g * 8, 8)
            kept[:, pl.ds(at, LANES)] = st_vel[pl.ds(to, 3), :]
        return carry

    lax.fori_loop(0, groups // 8, unstage, 0)

    chunk = 256
    lane_no = lax.broadcasted_iota(jnp.int32, (LANES, chunk), 0).astype(F32)
    iota_c = iota16[:, :chunk]
    for d in range(4):
        def pick(step, carry):
            at = pl.multiple_of(step * chunk, chunk)
            ids = mlist[d:d + 1, pl.ds(at, chunk)]
            hot = one_hot(spread16((ids // LANES).astype(F32)), groups, iota_c)
            here = lane_no == (ids % LANES).astype(F32)
            got = []
            for f in range(8):
                part = jnp.dot(gt_hi[f * LANES:(f + 1) * LANES, :], hot, preferred_element_type=F32)
                if f < 7:
                    part = part + jnp.dot(
                        gt_lo[f * LANES:(f + 1) * LANES, :], hot, preferred_element_type=F32
                    )
                got.append(jnp.sum(jnp.where(here, part, 0.0), axis=0, keepdims=True))
            gath[:, pl.ds(at, chunk)] = jnp.concatenate(got, axis=0)
            return carry

        lax.fori_loop(0, migs // chunk, pick, 0)
        g8 = gath[...]
        mov[d] = g8[4:7]
        h16 = spread16(g8[7:8])
        hits = [iota16 == h16 - float(16 * block) for block in range(LANES // 16)]
        pieces = []
        for f in range(4):
            pieces.append(parts_of(g8[f:f + 1]))
        for which in range(2):
            for f in range(4):
                v16 = spread16(pieces[f][which].astype(F32))
                for block in range(LANES // 16):
                    base = (which * 4 + f) * LANES + block * 16
                    b0[base:base + 16, :migs] = jnp.where(hits[block], v16, jnp.zeros((), BF16))
        slot_hot = one_hot(spread16(mslot[d:d + 1, :].astype(F32)), slots, iota16)
        block_rows = lax.dot_general(slot_hot, b0[:, :migs], NT, preferred_element_type=F32)
        rows[d, 0:slots, :] = block_rows[:, :4 * LANES] + block_rows[:, 4 * LANES:]
        ids = side[d:d + 1, :].astype(F32)
        rows[d, slots:slots + 8, :] = jnp.zeros((8, 4 * LANES), F32)
        rows[d, slots:slots + 1, d * slots:(d + 1) * slots] = ids
        rows[d, slots:slots + 1, (4 + d) * slots:(5 + d) * slots] = ids

    pl.semaphore_wait(barrier, 6)

    copies = []

    def send(source, target, send_sem, recv_sem, device):
        copy = pltpu.make_async_remote_copy(
            src_ref=source, dst_ref=target, send_sem=send_sem, recv_sem=recv_sem,
            device_id=device, device_id_type=MESH,
        )
        copy.start()
        copies.append(copy)
        return copy

    row_copies = [
        send(rows.at[d], got_rows.at[d], row_send.at[d], row_recv.at[d], near[d]) for d in range(4)
    ]

    sub = lax.broadcasted_iota(jnp.int32, (wide_y, LANES), 0)
    lane = lax.broadcasted_iota(jnp.int32, (wide_y, LANES), 1)

    def send_faces(phase, field, count):
        total = count * wide_x
        started = []
        started.append(send(
            field.at[:, 0], hx.at[phase, 1, pl.ds(0, count)],
            face_send.at[phase, 0], face_recv.at[phase, 1], near[0],
        ))
        started.append(send(
            field.at[:, wide_x - 1], hx.at[phase, 0, pl.ds(0, count)],
            face_send.at[phase, 1], face_recv.at[phase, 0], near[1],
        ))
        low = jnp.zeros((wide_y, LANES), F32)
        high = jnp.zeros((wide_y, LANES), F32)
        for j in range(total):
            plane = field[j // wide_x, j % wide_x]
            sy[phase, 0, j:j + 1, :] = plane[0:1, :]
            sy[phase, 1, j:j + 1, :] = plane[wide_y - 1:wide_y, :]
            low = jnp.where(lane == j, pltpu.roll(plane, j, 1) if j else plane, low)
            high = jnp.where(lane == j, pltpu.roll(plane, j + 1, 1), high)
        for side in range(2):
            started.append(send(
                sy.at[phase, side, pl.ds(0, total)], hy.at[phase, 1 - side, pl.ds(0, total)],
                face_send.at[phase, 2 + side], face_recv.at[phase, 3 - side], near[2 + side],
            ))
        sz[phase, 0] = low
        sz[phase, 1] = high
        for side in range(2):
            started.append(send(
                sz.at[phase, side], hz.at[phase, 1 - side],
                face_send.at[phase, 4 + side], face_recv.at[phase, 5 - side], near[4 + side],
            ))
        return started

    def arrive(started):
        for copy in started:
            copy.wait_recv()

    bottom = lax.axis_index("gz") == 0
    top = lax.axis_index("gz") == lax.axis_size("gz") - 1

    def z_halos(phase, wall):
        return (
            jnp.where(bottom, wall, hz[phase, 0]),
            jnp.where(top, wall, hz[phase, 1]),
        )

    def around(phase, field, c, x, z_low, z_high):
        j = c * wide_x + x
        here = field[c, x]
        x_low = field[c, x - 1] if x > 0 else hx[phase, 0, c]
        x_high = field[c, x + 1] if x < wide_x - 1 else hx[phase, 1, c]
        y_low = jnp.where(sub == 0, hy[phase, 0, j:j + 1, :], pltpu.roll(here, 1, 0))
        y_high = jnp.where(
            sub == wide_y - 1, hy[phase, 1, j:j + 1, :], pltpu.roll(here, wide_y - 1, 0)
        )
        edge_low = pltpu.roll(z_low, LANES - j, 1) if j else z_low
        edge_high = pltpu.roll(z_high, LANES - 1 - j, 1)
        below = jnp.where(lane == 0, edge_low, pltpu.roll(here, 1, 1))
        above = jnp.where(lane == LANES - 1, edge_high, pltpu.roll(here, LANES - 1, 1))
        return here, (x_low, x_high, y_low, y_high, below, above)

    first = send_faces(0, velocity, 3)
    mov_copies = [
        send(mov.at[d], got_mov.at[d], mov_send.at[d], mov_recv.at[d], near[d]) for d in range(4)
    ]

    cell_no = iota16[:, :LANES]
    height_no = jnp.stack([cell_no + float(16 * k) for k in range(LANES // 16)], axis=0)
    group_row_no = jnp.stack([cell_no + float(16 * k) for k in range(row_count // 16)], axis=0)
    nought, one = jnp.zeros((), BF16), jnp.ones((), BF16)

    def build(group0, b, a):
        for k in range(GROUP):
            g = group0 + k
            cols = slice(k * LANES, (k + 1) * LANES)
            hits = height_no == spread16(tabs[8, pl.ds(g, 1), :])[None]
            for p in range(8):
                v16 = spread16(tabs[p, pl.ds(g, 1), :])
                b[p * LANES:(p + 1) * LANES, cols] = jnp.where(hits, v16[None], nought).reshape(LANES, LANES)
            hits = group_row_no == spread16(tabs[9, pl.ds(g, 1), :])[None]
            a[:, cols] = jnp.where(hits, one, nought).reshape(row_count, LANES)

    def add(b, a):
        acc[...] += lax.dot_general(b[...], a[...], NT, preferred_element_type=F32)

    acc[...] = jnp.zeros_like(acc)
    build(0, b0, a0)
    pairs = groups // (2 * GROUP)

    def deposit(step, carry):
        build(step * 2 * GROUP + GROUP, b1, a1)
        add(b0, a0)
        build(jnp.minimum(step + 1, pairs - 1) * 2 * GROUP, b0, a0)
        add(b1, a1)
        return carry

    lax.fori_loop(0, pairs, deposit, 0)
    for f in range(4):
        total = acc[f * LANES:(f + 1) * LANES, :] + acc[(4 + f) * LANES:(5 + f) * LANES, :]
        dep[f] = total.T


    for d in range(4):
        row_copies[d].wait_recv()
    row_no = lax.broadcasted_iota(jnp.int32, (row_count, 8 * slots), 0).astype(F32)
    ids = sum(got_rows[d, slots:slots + 1, 0:8 * slots] for d in range(4))
    hot = jnp.where(row_no == ids, 1.0, 0.0).astype(BF16)
    pieces = [parts_of(got_rows[d, 0:slots, :]) for d in range(4)]
    depth = jnp.concatenate([p[0] for p in pieces] + [p[1] for p in pieces], axis=0)
    extra = jnp.dot(hot, depth, preferred_element_type=F32)
    fraction = 1.0 / (1.0 + (dep[3] + extra[:, 3 * LANES:]))
    phi[...] = fraction.reshape(1, wide_x, wide_y, LANES)
    second = send_faces(1, phi, 1)
    for c in range(3):
        drag = (dep[c] + extra[:, c * LANES:(c + 1) * LANES]).reshape(wide_x, wide_y, LANES)
        src[c] = phi[0] * velocity[c] - source_step * drag

    arrive(second)
    z_low, z_high = z_halos(1, 1.0)
    for x in range(wide_x):
        here, others = around(1, phi, 0, x, z_low, z_high)
        total = jnp.zeros_like(here)
        for k in range(6):
            weight = 0.5 * (here + others[k])
            wts[k, x] = weight
            total = total + weight
        inv[x] = 1.0 / (here + coupling * total)

    def sweep(phase, field, target):
        z_low, z_high = z_halos(phase, 0.0)
        for x in range(wide_x):
            for c in range(3):
                here, others = around(phase, field, c, x, z_low, z_high)
                flux = wts[0, x] * others[0]
                for k in range(1, 6):
                    flux = flux + wts[k, x] * others[k]
                target[c, x] = (src[c, x] + coupling * flux) * inv[x]

    arrive(first)
    sweep(0, velocity, u1)
    third = send_faces(2, u1, 3)
    for d in range(4):
        mov_copies[d].wait_recv()
        arrivals[d] = got_mov[d]
    arrive(third)
    sweep(2, u1, u2)
    fourth = send_faces(3, u2, 3)
    arrive(fourth)
    sweep(3, u2, out)
    for copy in copies:
        copy.wait_send()


def whole_step(
    velocity, fibre_vel, fluid_vel, fibre_props, fibre_row, fibre_height,
    migrant_list, migrant_slot, side_rows,
):
    _, wide_x, wide_y, wide_z = velocity.shape
    row_count = wide_x * wide_y
    fibres = fibre_vel.shape[1]
    groups = fibres // LANES
    migs = migrant_list.shape[1]
    slots = side_rows.shape[1]
    wide = GROUP * LANES
    vm = pl.BlockSpec(memory_space=pltpu.VMEM)
    sem = pltpu.SemaphoreType.DMA
    field = (3, wide_x, wide_y, wide_z)
    rows = (4, slots + 8, 4 * LANES)
    return pl.pallas_call(
        step_kernel,
        out_shape=(
            jax.ShapeDtypeStruct(velocity.shape, F32),
            jax.ShapeDtypeStruct((3, fibres), F32),
            jax.ShapeDtypeStruct((4, 3, migs), F32),
        ),
        in_specs=[vm] * 9,
        out_specs=(vm,) * 3,
        scratch_shapes=[
            pltpu.VMEM((groups * 8, LANES), F32),
            pltpu.VMEM((groups * 8, LANES), F32),
            pltpu.VMEM((groups * 8, LANES), F32),
            pltpu.VMEM((10, groups, LANES), F32),
            pltpu.VMEM((8 * LANES, groups), BF16),
            pltpu.VMEM((7 * LANES, groups), BF16),
            pltpu.VMEM((8, migs), F32),
            pltpu.VMEM((8 * LANES, wide), BF16),
            pltpu.VMEM((row_count, wide), BF16),
            pltpu.VMEM((8 * LANES, wide), BF16),
            pltpu.VMEM((row_count, wide), BF16),
            pltpu.VMEM((8 * LANES, row_count), F32),
            pltpu.VMEM((4, row_count, LANES), F32),
            pltpu.VMEM(rows, F32),
            pltpu.VMEM((4, 3, migs), F32),
            pltpu.VMEM(rows, F32),
            pltpu.VMEM((4, 3, migs), F32),
            pltpu.VMEM(field, F32),
            pltpu.VMEM(field, F32),
            pltpu.VMEM((1,) + field[1:], F32),
            pltpu.VMEM(field, F32),
            pltpu.VMEM((6,) + field[1:], F32),
            pltpu.VMEM(field[1:], F32),
            pltpu.VMEM((4, 2, 3 * wide_x, wide_z), F32),
            pltpu.VMEM((4, 2, wide_y, wide_z), F32),
            pltpu.VMEM((4, 2, 3, wide_y, wide_z), F32),
            pltpu.VMEM((4, 2, 3 * wide_x, wide_z), F32),
            pltpu.VMEM((4, 2, wide_y, wide_z), F32),
            sem((4,)), sem((4,)), sem((4,)), sem((4,)), sem((4, 6)), sem((4, 6)),
        ],
        compiler_params=pltpu.CompilerParams(
            collective_id=0, has_side_effects=True, vmem_limit_bytes=56 * 1024 * 1024
        ),
        cost_estimate=pl.CostEstimate(flops=24_000_000_000, bytes_accessed=3_000_000, transcendentals=0),
        name="step",
    )(
        velocity, fibre_vel, fluid_vel, fibre_props,
        fibre_row.reshape(groups, LANES), fibre_height.reshape(groups, LANES),
        migrant_list, migrant_slot, side_rows,
    )


def body(*args):
    return whole_step(*args)


def solution(mesh):
    placed = (
        P(None, "gx", "gy", "gz"),
        P(None, ("gx", "gy", "gz")),
        P(None, ("gx", "gy", "gz")),
        P(None, ("gx", "gy", "gz")),
        P(("gx", "gy", "gz")),
        P(("gx", "gy", "gz")),
        P(None, ("gx", "gy", "gz")),
        P(None, ("gx", "gy", "gz")),
        P(None, ("gx", "gy", "gz")),
    )
    return jax.shard_map(
        body,
        mesh=mesh,
        in_specs=placed,
        out_specs=(
            P(None, "gx", "gy", "gz"),
            P(None, ("gx", "gy", "gz")),
            P(None, None, ("gx", "gy", "gz")),
        ),
        check_vma=False,
    )
```

```python
import jax
import jax.numpy as jnp
from jax import lax
from jax.experimental import pallas as pl
from jax.experimental.pallas import tpu as pltpu
from jax.sharding import PartitionSpec as P

SWEEPS = 3
drag_step = 0.25
source_step = 1.0
coupling = 1.0
F32, BF16 = jnp.float32, jnp.bfloat16
LANES = 128
GROUP = 16
NT = (((1,), (1,)), ((), ()))


def parts_of(value):
    high = value.astype(BF16)
    low = (value - high.astype(F32)).astype(BF16)
    return high, low


def spread16(row):
    return jnp.broadcast_to(row, (16, row.shape[1])).astype(BF16)


def one_hot(row16, count, iota16):
    blocks = count // 16
    n = row16.shape[1]
    out = []
    for block in range(blocks):
        hit = iota16 == row16 - float(block * 16)
        out.append(jnp.where(hit, jnp.ones((), BF16), jnp.zeros((), BF16)))
    return jnp.concatenate(out, axis=0)


def local_kernel(
    vel, flu, prop, row, height, mlist, mslot, side,
    kept, dep, rows, mov,
    st_vel, st_flu, st_prop, tabs, moved_t, gt_hi, gt_lo, gath, b0, a0, b1, a1, acc,
):
    groups = row.shape[0]
    row_count = dep.shape[1]
    migs = mlist.shape[1]
    slots = side.shape[1]

    def stage(step, carry):
        for k in range(8):
            g = step * 8 + k
            at = pl.multiple_of(g * LANES, LANES)
            to = pl.multiple_of(g * 8, 8)
            st_vel[pl.ds(to, 3), :] = vel[:, pl.ds(at, LANES)]
            st_flu[pl.ds(to, 3), :] = flu[:, pl.ds(at, LANES)]
            st_prop[pl.ds(to, 2), :] = prop[:, pl.ds(at, LANES)]
        return carry

    lax.fori_loop(0, groups // 8, stage, 0)

    lists = mlist[...]
    list_hi = (lists // LANES).astype(F32)
    list_lo = (lists % LANES).astype(F32)
    iota16 = lax.broadcasted_iota(jnp.int32, (16, migs), 0).astype(F32).astype(BF16)
    named = jnp.zeros((groups, LANES), F32)
    for d in range(4):
        named = named + lax.dot_general(
            one_hot(spread16(list_hi[d:d + 1]), groups, iota16),
            one_hot(spread16(list_lo[d:d + 1]), LANES, iota16),
            NT, preferred_element_type=F32,
        )
    leaves = named > 0.5

    volume = st_prop[pl.ds(0, groups, stride=8), :]
    beta = st_prop[pl.ds(1, groups, stride=8), :]
    for c in range(3):
        v = st_vel[pl.ds(c, groups, stride=8), :]
        f = st_flu[pl.ds(c, groups, stride=8), :]
        force = beta * (f - v)
        moved = v + drag_step * force / volume
        st_vel[pl.ds(c, groups, stride=8), :] = jnp.where(leaves, 0.0, moved)
        hi, lo = parts_of(force)
        tabs[c] = hi.astype(F32)
        tabs[4 + c] = lo.astype(F32)
        moved_t[c] = moved
        hi, lo = parts_of(force.T)
        gt_hi[c * LANES:(c + 1) * LANES, :] = hi
        gt_lo[c * LANES:(c + 1) * LANES, :] = lo
        hi, lo = parts_of(moved.T)
        gt_hi[(4 + c) * LANES:(5 + c) * LANES, :] = hi
        gt_lo[(4 + c) * LANES:(5 + c) * LANES, :] = lo
    hi, lo = parts_of(volume)
    tabs[3] = hi.astype(F32)
    tabs[7] = lo.astype(F32)
    hi, lo = parts_of(volume.T)
    gt_hi[3 * LANES:4 * LANES, :] = hi
    gt_lo[3 * LANES:4 * LANES, :] = lo
    hgt = height[...].astype(F32)
    tabs[8] = hgt
    tabs[9] = jnp.where(leaves, -1.0, row[...].astype(F32))
    gt_hi[7 * LANES:8 * LANES, :] = hgt.T.astype(BF16)

    def unstage(step, carry):
        for k in range(8):
            g = step * 8 + k
            at = pl.multiple_of(g * LANES, LANES)
            to = pl.multiple_of(g * 8, 8)
            kept[:, pl.ds(at, LANES)] = st_vel[pl.ds(to, 3), :]
        return carry

    lax.fori_loop(0, groups // 8, unstage, 0)

    chunk = 256
    lane_no = lax.broadcasted_iota(jnp.int32, (LANES, chunk), 0).astype(F32)
    iota_c = iota16[:, :chunk]
    for d in range(4):
        def pick(step, carry):
            at = pl.multiple_of(step * chunk, chunk)
            ids = mlist[d:d + 1, pl.ds(at, chunk)]
            hot = one_hot(spread16((ids // LANES).astype(F32)), groups, iota_c)
            here = lane_no == (ids % LANES).astype(F32)
            whole = jnp.dot(gt_hi[...], hot, preferred_element_type=F32)
            low = jnp.dot(gt_lo[...], hot, preferred_element_type=F32)
            got = []
            for f in range(8):
                part = whole[f * LANES:(f + 1) * LANES]
                if f < 7:
                    part = part + low[f * LANES:(f + 1) * LANES]
                got.append(jnp.sum(jnp.where(here, part, 0.0), axis=0, keepdims=True))
            gath[:, pl.ds(at, chunk)] = jnp.concatenate(got, axis=0)
            return carry

        lax.fori_loop(0, migs // chunk, pick, 0)
        g8 = gath[...]
        mov[d] = g8[4:7]
        h16 = spread16(g8[7:8])
        hits = [iota16 == h16 - float(16 * block) for block in range(LANES // 16)]
        pieces = []
        for f in range(4):
            pieces.append(parts_of(g8[f:f + 1]))
        for which in range(2):
            for f in range(4):
                v16 = spread16(pieces[f][which].astype(F32))
                for block in range(LANES // 16):
                    base = (which * 4 + f) * LANES + block * 16
                    b0[base:base + 16, :migs] = jnp.where(hits[block], v16, jnp.zeros((), BF16))
        slot_hot = one_hot(spread16(mslot[d:d + 1, :].astype(F32)), slots, iota16)
        block_rows = lax.dot_general(slot_hot, b0[:, :migs], NT, preferred_element_type=F32)
        rows[d, 0:slots, :] = block_rows[:, :4 * LANES] + block_rows[:, 4 * LANES:]
        ids = side[d:d + 1, :].astype(F32)
        rows[d, slots:slots + 8, :] = jnp.zeros((8, 4 * LANES), F32)
        rows[d, slots:slots + 1, d * slots:(d + 1) * slots] = ids
        rows[d, slots:slots + 1, (4 + d) * slots:(5 + d) * slots] = ids

    cell_no = iota16[:, :LANES]
    height_no = jnp.stack([cell_no + float(16 * k) for k in range(LANES // 16)], axis=0)
    group_row_no = jnp.stack([cell_no + float(16 * k) for k in range(row_count // 16)], axis=0)
    nought, one = jnp.zeros((), BF16), jnp.ones((), BF16)

    def build(group0, b, a):
        for k in range(GROUP):
            g = group0 + k
            cols = slice(k * LANES, (k + 1) * LANES)
            hits = height_no == spread16(tabs[8, pl.ds(g, 1), :])[None]
            for p in range(8):
                v16 = spread16(tabs[p, pl.ds(g, 1), :])
                b[p * LANES:(p + 1) * LANES, cols] = jnp.where(hits, v16[None], nought).reshape(LANES, LANES)
            hits = group_row_no == spread16(tabs[9, pl.ds(g, 1), :])[None]
            a[:, cols] = jnp.where(hits, one, nought).reshape(row_count, LANES)

    def add(b, a):
        acc[...] += lax.dot_general(b[...], a[...], NT, preferred_element_type=F32)

    acc[...] = jnp.zeros_like(acc)
    build(0, b0, a0)
    pairs = groups // (2 * GROUP)

    def deposit(step, carry):
        build(step * 2 * GROUP + GROUP, b1, a1)
        add(b0, a0)
        build(jnp.minimum(step + 1, pairs - 1) * 2 * GROUP, b0, a0)
        add(b1, a1)
        return carry

    lax.fori_loop(0, pairs, deposit, 0)
    for f in range(4):
        total = acc[f * LANES:(f + 1) * LANES, :] + acc[(4 + f) * LANES:(5 + f) * LANES, :]
        dep[f] = total.T


def local_part(fibre_vel, fluid_vel, fibre_props, fibre_row, fibre_height, migrant_list, migrant_slot, side_rows, row_count):
    fibres = fibre_vel.shape[1]
    groups = fibres // LANES
    migs = migrant_list.shape[1]
    slots = side_rows.shape[1]
    wide = GROUP * LANES
    vm = pl.BlockSpec(memory_space=pltpu.VMEM)
    return pl.pallas_call(
        local_kernel,
        out_shape=(
            jax.ShapeDtypeStruct((3, fibres), F32),
            jax.ShapeDtypeStruct((4, row_count, LANES), F32),
            jax.ShapeDtypeStruct((4, slots + 8, 4 * LANES), F32),
            jax.ShapeDtypeStruct((4, 3, migs), F32),
        ),
        in_specs=[vm] * 8,
        out_specs=(vm,) * 4,
        scratch_shapes=[
            pltpu.VMEM((groups * 8, LANES), F32),
            pltpu.VMEM((groups * 8, LANES), F32),
            pltpu.VMEM((groups * 8, LANES), F32),
            pltpu.VMEM((10, groups, LANES), F32),
            pltpu.VMEM((3, groups, LANES), F32),
            pltpu.VMEM((8 * LANES, groups), BF16),
            pltpu.VMEM((7 * LANES, groups), BF16),
            pltpu.VMEM((8, migs), F32),
            pltpu.VMEM((8 * LANES, wide), BF16),
            pltpu.VMEM((row_count, wide), BF16),
            pltpu.VMEM((8 * LANES, wide), BF16),
            pltpu.VMEM((row_count, wide), BF16),
            pltpu.VMEM((8 * LANES, row_count), F32),
        ],
        compiler_params=pltpu.CompilerParams(vmem_limit_bytes=56 * 1024 * 1024),
        cost_estimate=pl.CostEstimate(flops=17_000_000_000, bytes_accessed=3_000_000, transcendentals=0),
        name="fibres",
    )(
        fibre_vel, fluid_vel, fibre_props,
        fibre_row.reshape(groups, LANES), fibre_height.reshape(groups, LANES),
        migrant_list, migrant_slot, side_rows,
    )


MESH = pl.DeviceIdType.MESH


def sweep_kernel(
    velocity, dep, rows, mov,
    out, arrivals,
    got_rows, got_mov, u1, u2, phi, src, wts, inv, sy, sz, hx, hy, hz,
    row_send, row_recv, mov_send, mov_recv, face_send, face_recv,
):
    wide_x, wide_y = velocity.shape[1], velocity.shape[2]
    slots = rows.shape[1] - 8
    near = []
    for axis in ("gx", "gy", "gz"):
        n = lax.axis_size(axis)
        me = lax.axis_index(axis)
        near.append({axis: lax.rem(me + n - 1, n)})
        near.append({axis: lax.rem(me + 1, n)})

    barrier = pltpu.get_barrier_semaphore()
    for device in near:
        pl.semaphore_signal(barrier, inc=1, device_id=device, device_id_type=MESH)
    pl.semaphore_wait(barrier, 6)

    copies = []

    def send(source, target, send_sem, recv_sem, device):
        copy = pltpu.make_async_remote_copy(
            src_ref=source, dst_ref=target, send_sem=send_sem, recv_sem=recv_sem,
            device_id=device, device_id_type=MESH,
        )
        copy.start()
        copies.append(copy)
        return copy

    row_copies = [
        send(rows.at[d], got_rows.at[d], row_send.at[d], row_recv.at[d], near[d]) for d in range(4)
    ]

    sub = lax.broadcasted_iota(jnp.int32, (wide_y, LANES), 0)
    lane = lax.broadcasted_iota(jnp.int32, (wide_y, LANES), 1)

    def send_faces(phase, field, count):
        total = count * wide_x
        started = []
        started.append(send(
            field.at[:, 0], hx.at[phase, 1, pl.ds(0, count)],
            face_send.at[phase, 0], face_recv.at[phase, 1], near[0],
        ))
        started.append(send(
            field.at[:, wide_x - 1], hx.at[phase, 0, pl.ds(0, count)],
            face_send.at[phase, 1], face_recv.at[phase, 0], near[1],
        ))
        low = jnp.zeros((wide_y, LANES), F32)
        high = jnp.zeros((wide_y, LANES), F32)
        for j in range(total):
            plane = field[j // wide_x, j % wide_x]
            sy[phase, 0, j:j + 1, :] = plane[0:1, :]
            sy[phase, 1, j:j + 1, :] = plane[wide_y - 1:wide_y, :]
            low = jnp.where(lane == j, pltpu.roll(plane, j, 1) if j else plane, low)
            high = jnp.where(lane == j, pltpu.roll(plane, j + 1, 1), high)
        for side in range(2):
            started.append(send(
                sy.at[phase, side, pl.ds(0, total)], hy.at[phase, 1 - side, pl.ds(0, total)],
                face_send.at[phase, 2 + side], face_recv.at[phase, 3 - side], near[2 + side],
            ))
        sz[phase, 0] = low
        sz[phase, 1] = high
        for side in range(2):
            started.append(send(
                sz.at[phase, side], hz.at[phase, 1 - side],
                face_send.at[phase, 4 + side], face_recv.at[phase, 5 - side], near[4 + side],
            ))
        return started

    def arrive(started):
        for copy in started:
            copy.wait_recv()

    bottom = lax.axis_index("gz") == 0
    top = lax.axis_index("gz") == lax.axis_size("gz") - 1

    def z_halos(phase, wall):
        return (
            jnp.where(bottom, wall, hz[phase, 0]),
            jnp.where(top, wall, hz[phase, 1]),
        )

    def around(phase, field, c, x, z_low, z_high):
        j = c * wide_x + x
        here = field[c, x]
        x_low = field[c, x - 1] if x > 0 else hx[phase, 0, c]
        x_high = field[c, x + 1] if x < wide_x - 1 else hx[phase, 1, c]
        y_low = jnp.where(sub == 0, hy[phase, 0, j:j + 1, :], pltpu.roll(here, 1, 0))
        y_high = jnp.where(
            sub == wide_y - 1, hy[phase, 1, j:j + 1, :], pltpu.roll(here, wide_y - 1, 0)
        )
        edge_low = pltpu.roll(z_low, LANES - j, 1) if j else z_low
        edge_high = pltpu.roll(z_high, LANES - 1 - j, 1)
        below = jnp.where(lane == 0, edge_low, pltpu.roll(here, 1, 1))
        above = jnp.where(lane == LANES - 1, edge_high, pltpu.roll(here, LANES - 1, 1))
        return here, (x_low, x_high, y_low, y_high, below, above)

    first = send_faces(0, velocity, 3)
    mov_copies = [
        send(mov.at[d], got_mov.at[d], mov_send.at[d], mov_recv.at[d], near[d]) for d in range(4)
    ]

    for d in range(4):
        row_copies[d].wait_recv()
    row_no = lax.broadcasted_iota(jnp.int32, (wide_x * wide_y, 8 * slots), 0).astype(F32)
    ids = sum(got_rows[d, slots:slots + 1, 0:8 * slots] for d in range(4))
    hot = jnp.where(row_no == ids, 1.0, 0.0).astype(BF16)
    pieces = [parts_of(got_rows[d, 0:slots, :]) for d in range(4)]
    depth = jnp.concatenate([p[0] for p in pieces] + [p[1] for p in pieces], axis=0)
    extra = jnp.dot(hot, depth, preferred_element_type=F32)
    fraction = 1.0 / (1.0 + (dep[3] + extra[:, 3 * LANES:]))
    phi[...] = fraction.reshape(1, wide_x, wide_y, LANES)
    second = send_faces(1, phi, 1)
    for c in range(3):
        drag = (dep[c] + extra[:, c * LANES:(c + 1) * LANES]).reshape(wide_x, wide_y, LANES)
        src[c] = phi[0] * velocity[c] - source_step * drag

    arrive(second)
    z_low, z_high = z_halos(1, 1.0)
    for x in range(wide_x):
        here, others = around(1, phi, 0, x, z_low, z_high)
        total = jnp.zeros_like(here)
        for k in range(6):
            weight = 0.5 * (here + others[k])
            wts[k, x] = weight
            total = total + weight
        inv[x] = 1.0 / (here + coupling * total)

    def sweep(phase, field, target):
        z_low, z_high = z_halos(phase, 0.0)
        for x in range(wide_x):
            for c in range(3):
                here, others = around(phase, field, c, x, z_low, z_high)
                flux = wts[0, x] * others[0]
                for k in range(1, 6):
                    flux = flux + wts[k, x] * others[k]
                target[c, x] = (src[c, x] + coupling * flux) * inv[x]

    arrive(first)
    sweep(0, velocity, u1)
    third = send_faces(2, u1, 3)
    for d in range(4):
        mov_copies[d].wait_recv()
        arrivals[d] = got_mov[d]
    arrive(third)
    sweep(2, u1, u2)
    fourth = send_faces(3, u2, 3)
    arrive(fourth)
    sweep(3, u2, out)
    for copy in copies:
        copy.wait_send()


def sweeps(velocity, deposit, rows, movers):
    _, wide_x, wide_y, wide_z = velocity.shape
    vm = pl.BlockSpec(memory_space=pltpu.VMEM)
    sem = pltpu.SemaphoreType.DMA
    field = (3, wide_x, wide_y, wide_z)
    return pl.pallas_call(
        sweep_kernel,
        out_shape=(
            jax.ShapeDtypeStruct(velocity.shape, F32),
            jax.ShapeDtypeStruct(movers.shape, F32),
        ),
        in_specs=[vm] * 4,
        out_specs=(vm,) * 2,
        scratch_shapes=[
            pltpu.VMEM(rows.shape, F32),
            pltpu.VMEM(movers.shape, F32),
            pltpu.VMEM(field, F32),
            pltpu.VMEM(field, F32),
            pltpu.VMEM((1,) + field[1:], F32),
            pltpu.VMEM(field, F32),
            pltpu.VMEM((6,) + field[1:], F32),
            pltpu.VMEM(field[1:], F32),
            pltpu.VMEM((4, 2, 3 * wide_x, wide_z), F32),
            pltpu.VMEM((4, 2, wide_y, wide_z), F32),
            pltpu.VMEM((4, 2, 3, wide_y, wide_z), F32),
            pltpu.VMEM((4, 2, 3 * wide_x, wide_z), F32),
            pltpu.VMEM((4, 2, wide_y, wide_z), F32),
            sem((4,)), sem((4,)), sem((4,)), sem((4,)), sem((4, 6)), sem((4, 6)),
        ],
        compiler_params=pltpu.CompilerParams(
            collective_id=0, has_side_effects=True, vmem_limit_bytes=32 * 1024 * 1024
        ),
        cost_estimate=pl.CostEstimate(flops=20_000_000, bytes_accessed=2_000_000, transcendentals=0),
        name="sweeps",
    )(velocity, deposit, rows, movers)


def body(
    velocity, fibre_vel, fluid_vel, fibre_props, fibre_row, fibre_height,
    migrant_list, migrant_slot, side_rows,
):
    row_count = velocity.shape[1] * velocity.shape[2]
    kept_fibres, deposit, rows, movers = local_part(
        fibre_vel, fluid_vel, fibre_props, fibre_row, fibre_height,
        migrant_list, migrant_slot, side_rows, row_count,
    )
    new_velocity, arrivals = sweeps(velocity, deposit, rows, movers)
    return new_velocity, kept_fibres, arrivals


def solution(mesh):
    placed = (
        P(None, "gx", "gy", "gz"),
        P(None, ("gx", "gy", "gz")),
        P(None, ("gx", "gy", "gz")),
        P(None, ("gx", "gy", "gz")),
        P(("gx", "gy", "gz")),
        P(("gx", "gy", "gz")),
        P(None, ("gx", "gy", "gz")),
        P(None, ("gx", "gy", "gz")),
        P(None, ("gx", "gy", "gz")),
    )
    return jax.shard_map(
        body,
        mesh=mesh,
        in_specs=placed,
        out_specs=(
            P(None, "gx", "gy", "gz"),
            P(None, ("gx", "gy", "gz")),
            P(None, None, ("gx", "gy", "gz")),
        ),
        check_vma=False,
    )
```
